32 devices in a mesh: rows: 8 (over y, x, core), feat: 4 (over z).
Axes of the slice: x: 2, y: 2, z: 4, core: 2. Of those that a mesh axis runs over, the one named last changes fastest.
Arguments:
- features: bfloat16 [16384, 512], P(('rows', 'feat')), may hold values from -6 to 6
- weight: bfloat16 [512, 512], replicated, may hold values from -0.25 to 0.25
- layer_bias: float32 [512], replicated, may hold values from -3 to 3
- block_cols: int32 [128, 6], P(('rows', 'feat')), may hold values from 0 to 127, as said below
- neighbours: int32 [16384, 30], P(('rows', 'feat')), may hold values from 0 to 767
- row_counts: int32 [16384], P(('rows', 'feat')), may hold values from 1 to 30
- out_grad: bfloat16 [16384, 512], P(('rows', 'feat')), may hold values from -6 to 6
Outputs:
- hidden: bfloat16 [16384, 512], P(('rows', 'feat'))
- input_grad: bfloat16 [16384, 512], P(('rows', 'feat'))
- weight_grad: float32 [512, 512], P('rows')
- bias_grad: float32 [512], P('rows')
The draws below stay inside these ranges and needn't reach their ends.
Inputs may be any that keep to these rules, and one draw needn't show every extreme that they name: `block_cols`: block row t is node rows 128 * t to 128 * t + 127. With g = (t // 4) * 4: slot 0 is t itself, slot 1 lies in tiles g - 4 to g - 1, slot 2 in tiles g + 4 to g + 2 * 4 - 1, and every slot in tiles g - 4 to g + 2 * 4 - 1, all taken modulo 128. `neighbours`: entries at positions row_counts or later are unused.
All inputs are finite; a program needn't handle non-finite values.
Results may differ from the reference program's by a relative error of at most 0.0095.
Values may be sent and summed in bfloat16 or wider, within the bound.
A program may use at most 64 MiB of HBM per device.

```python
import math
import jax
import jax.numpy as jnp
from jax import lax

F = 512
K = 30
BLK = 128
MAXB = 6
TILE_DEV = 4
NTILES = 128
NODES = 16384


def draw_block_cols(key, part):
    first_key, second_key, third_key = jax.random.split(key, 3)
    tile_ids = jnp.arange(NTILES, dtype=jnp.int32)
    group_start = tile_ids // TILE_DEV * TILE_DEV
    own_place = tile_ids - group_start + TILE_DEV
    lower_pick = jax.random.randint(first_key, (NTILES, 1), 0, TILE_DEV, dtype=jnp.int32)
    upper_pick = jax.random.randint(second_key, (NTILES, 1), 0, TILE_DEV, dtype=jnp.int32) + 2 * TILE_DEV
    other_pick = jax.random.randint(third_key, (NTILES, MAXB - 3), 0, 3 * TILE_DEV, dtype=jnp.int32)
    places = jnp.concatenate([own_place[:, None], lower_pick, upper_pick, other_pick], axis=1)
    return jnp.mod(group_start[:, None] - TILE_DEV + places, NTILES).astype(jnp.int32)


def set_ends(result, stream_key, smallest, largest):
    spot = [jax.random.randint(jax.random.fold_in(stream_key, axis), (), 0, length) for axis, length in enumerate(result.shape)]
    main_axis = result.shape.index(max(result.shape))
    next_to = spot[:main_axis] + [(spot[main_axis] + 1) % result.shape[main_axis]] + spot[main_axis + 1:]
    return result.at[tuple(spot)].set(smallest).at[tuple(next_to)].set(largest)


def raised(array, rng, source, target, parts, factor):
    def block_of(axis_at):
        return (jnp.arange(array.shape[axis_at]) // (array.shape[axis_at] // parts)).reshape((-1,) + (1,) * (array.ndim - 1 - axis_at))

    first = jax.random.permutation(rng, parts)[block_of(target)]
    second = (block_of(target) + parts // 2) % parts
    return jnp.where((block_of(source) == first) | (block_of(source) == second), factor * array, array)


def steps_of(key, dims, cuts, smallest, largest):
    def one(position, blocks):
        draws = jax.random.uniform(jax.random.fold_in(jax.random.fold_in(key, 6), position), (blocks,), jnp.float32, smallest / len(cuts), largest / len(cuts))
        return jnp.repeat(jnp.exp(draws), dims[position] // blocks).reshape((-1,) + (1,) * (len(dims) - position - 1))

    loudness = one(*cuts[0])
    for cut in cuts[1:]:
        loudness = loudness * one(*cut)
    return loudness


def noise(key, dims, deviation, reach, cuts=(), kind=jnp.bfloat16):
    result = deviation * jax.random.normal(key, dims, jnp.float32)
    if cuts:
        result = result * steps_of(key, dims, cuts, -0.22, 0.18)
    return jnp.clip(result, -reach, reach).astype(kind)


def bell_draw_with(own_key, shape, scale, bound, cuts, heavy, held_as=jnp.bfloat16):
    result = scale * jax.random.normal(own_key, shape, jnp.float32)
    if cuts:
        result = result * steps_of(own_key, shape, cuts, -0.22, 0.18)
    return jnp.clip(raised(result, jax.random.fold_in(own_key, 3), *heavy), -bound, bound).astype(held_as)


def setup_inputs(seed: int = 0) -> dict:
    seeds = jax.random.split(jax.random.key(seed), 8)
    return {
        "features": bell_draw_with(seeds[0], (NODES, F), 1.0, 6.0, ((0, 32),), (0, 1, 32, 2.75)),
        "weight": noise(seeds[1], (F, F), F ** -0.5, 0.25),
        "layer_bias": noise(seeds[2], (F,), 0.5, 3.0, (), jnp.float32),
        "block_cols": draw_block_cols(jax.random.fold_in(seeds[7], 71), 0),
        "neighbours": set_ends(jax.random.randint(seeds[4], (NODES, K), 0, MAXB * BLK), jax.random.fold_in(seeds[4], 1), 0, (MAXB * BLK) - 1).astype(jnp.int32),
        "row_counts": set_ends(jax.random.randint(seeds[5], (NODES,), 1, K + 1), jax.random.fold_in(seeds[5], 1), 1, K).astype(jnp.int32),
        "out_grad": bell_draw_with(seeds[6], (NODES, F), 1.0, 6.0, ((0, 32),), (0, 1, 32, 2.75)),
    }


def strip_counts(neighbours, row_counts, strip_width):
    columns = jnp.arange(strip_width, dtype=jnp.int32)
    slot_ids = jnp.arange(neighbours.shape[1], dtype=jnp.int32)
    live_slot = slot_ids[None, :] < row_counts[:, None]
    matches = (neighbours[:, :, None] == columns[None, None, :]) & live_slot[:, :, None]
    return lax.optimization_barrier(jnp.sum(matches.astype(jnp.int32), axis=1)).astype(jnp.bfloat16)

def reference(features, weight, layer_bias, block_cols, neighbours, row_counts, out_grad):
    feat_width = features.shape[1]
    tile_total = block_cols.shape[0]
    normaliser = 1.0 / math.sqrt(NODES)
    inverse_root = lax.rsqrt(1.0 + row_counts.astype(jnp.float32))[:, None]
    projected = jnp.dot(features, weight, preferred_element_type=jnp.float32)
    proj_scaled = (projected * inverse_root).astype(jnp.bfloat16)
    scaled_tiles = proj_scaled.reshape(tile_total, BLK, feat_width)
    nbr_tiles = neighbours.reshape(tile_total, BLK, K)
    count_tiles = row_counts.reshape(tile_total, BLK)

    def forward_tile(operands):
        tile_cols, tile_nbr, tile_cnt = operands
        count_strip = strip_counts(tile_nbr, tile_cnt, MAXB * BLK)
        sources = scaled_tiles[tile_cols.astype(jnp.int32)].reshape(MAXB * BLK, feat_width)
        return jnp.dot(count_strip, sources, preferred_element_type=jnp.float32)
    summed = lax.map(forward_tile, (block_cols, nbr_tiles, count_tiles)).reshape(NODES, feat_width)
    pre_activation = inverse_root * (summed + proj_scaled.astype(jnp.float32)) + layer_bias[None, :]
    sigmoid_gate = jax.nn.sigmoid(pre_activation)
    hidden = (pre_activation * sigmoid_gate).astype(jnp.bfloat16)
    grad_pre = out_grad.astype(jnp.float32) * sigmoid_gate * (1.0 + pre_activation * (1.0 - sigmoid_gate))
    grad_scaled = (grad_pre * inverse_root).astype(jnp.bfloat16)
    grad_tiles = grad_scaled.reshape(tile_total, BLK, feat_width)

    def backward_tile(carried, operands):
        tile_cols, tile_nbr, tile_cnt, tile_grad = operands
        count_strip = strip_counts(tile_nbr, tile_cnt, MAXB * BLK)
        contribution = lax.dot_general(count_strip, tile_grad, (((0,), (0,)), ((), ())), preferred_element_type=jnp.float32)
        contribution = contribution.reshape(MAXB, BLK, feat_width)
        return (carried.at[tile_cols.astype(jnp.int32)].add(contribution), None)
    initial = jnp.zeros((tile_total, BLK, feat_width), jnp.float32)
    gathered, _ = lax.scan(backward_tile, initial, (block_cols, nbr_tiles, count_tiles, grad_tiles))
    gathered = gathered.reshape(NODES, feat_width)
    grad_proj = (inverse_root * (gathered + grad_scaled.astype(jnp.float32))).astype(jnp.bfloat16)
    input_grad = lax.dot_general(grad_proj, weight, (((1,), (1,)), ((), ())), preferred_element_type=jnp.float32).astype(jnp.bfloat16)
    weight_grad = lax.dot_general(features, grad_proj, (((0,), (0,)), ((), ())), preferred_element_type=jnp.float32) * normaliser
    bias_grad = lax.optimization_barrier(jnp.sum(grad_pre, axis=0)) * normaliser
    return (hidden, input_grad, weight_grad, bias_grad)
```

```python
import functools
import math

import jax
import jax.numpy as jnp
from jax import lax
from jax.experimental import pallas as pl
from jax.experimental.pallas import tpu as pltpu
from jax.sharding import PartitionSpec as P

LANES = 128
GROUP = 16
f32 = jnp.float32
bf16 = jnp.bfloat16


def matmul(a, b):
    return jnp.dot(a, b, preferred_element_type=f32)


def kernel(
    rows_n, feat_n, scale,
    features, weight, bias, out_grad, keys, inverse_root,
    hidden, input_grad, weight_grad, bias_grad,
    window, adj, adj_t, features_t, part_out, part_in, own, grad_proj,
    wsend, wrecv, zbuf, bsend, brecv, bz,
    fwd_send, fwd_recv, bwd_send, bwd_recv, ws_sem, wr_sem, zs_sem, zr_sem,
    bs_sem, br_sem, bzs_sem, bzr_sem,
):
    n = features.shape[0]
    chunks = window.shape[0]
    share = weight_grad.shape[0]
    r = lax.axis_index("rows")
    z = lax.axis_index("feat")
    count = rows_n * feat_n
    me = r * feat_n + z
    prev = lax.rem(me + count - 1, count)
    succ = lax.rem(me + 1, count)
    sides = (
        {"rows": lax.div(prev, feat_n), "feat": lax.rem(prev, feat_n)},
        {"rows": lax.div(succ, feat_n), "feat": lax.rem(succ, feat_n)},
    )

    def row_peer(d):
        return {"rows": lax.rem(r + d, rows_n), "feat": z}

    def feat_peer(d):
        return {"rows": r, "feat": lax.rem(z + d, feat_n)}

    def remote(src, dst, send, recv, device):
        return pltpu.make_async_remote_copy(
            src_ref=src, dst_ref=dst, send_sem=send, recv_sem=recv,
            device_id=device, device_id_type=pl.DeviceIdType.MESH,
        )

    def each(size, act):
        def body(d, carry):
            act(d)
            return carry
        lax.fori_loop(1, size, body, 0)

    def cols(c):
        return pl.ds(c * LANES, LANES)

    def fwd(side, c):
        place = pl.ds(2 * n if side == 0 else 0, n)
        return remote(
            window.at[c, pl.ds(n, n)], window.at[c, place],
            fwd_send.at[side, c], fwd_recv.at[side, c], sides[side],
        )

    def bwd(side, c):
        return remote(
            part_out.at[side, c], part_in.at[side, c],
            bwd_send.at[side, c], bwd_recv.at[side, c], sides[side],
        )

    def wcopy(c, d):
        peer = row_peer(d)
        start = pl.multiple_of(peer["rows"] * share, share)
        return remote(
            wsend.at[c, pl.ds(start, share)], wrecv.at[c, d], ws_sem.at[c, d], wr_sem.at[c, d], peer
        )

    def zcopy(c, d):
        return remote(zbuf.at[c, z], zbuf.at[c, z], zs_sem.at[c, d], zr_sem.at[c, d], feat_peer(d))

    def bcopy(d):
        return remote(bsend, brecv.at[d], bs_sem.at[d], br_sem.at[d], row_peer(d))

    def bzcopy(d):
        return remote(bz.at[z], bz.at[z], bzs_sem.at[d], bzr_sem.at[d], feat_peer(d))

    barrier = pltpu.get_barrier_semaphore()

    def greet(device):
        pl.semaphore_signal(
            barrier, inc=1, device_id=device, device_id_type=pl.DeviceIdType.MESH
        )

    greet(sides[0])
    greet(sides[1])
    each(rows_n, lambda d: greet(row_peer(d)))
    each(feat_n, lambda d: greet(feat_peer(d)))

    for c in range(chunks):
        product = matmul(features[...], weight[:, cols(c)])
        window[c, pl.ds(n, n), :] = (product * inverse_root[...]).astype(bf16)
        if c == 0:
            pl.semaphore_wait(barrier, rows_n + feat_n)
        fwd(0, c).start()
        fwd(1, c).start()

    features_t[...] = features[...].T
    columns = lax.broadcasted_iota(jnp.int32, (GROUP, 3 * n), 1)

    def fill(g, carry):
        at = pl.ds(pl.multiple_of(g * GROUP, GROUP), GROUP)
        mine = keys[at, :]
        total = jnp.zeros((GROUP, 3 * n), jnp.int32)
        for k in range(keys.shape[1]):
            total = total + (mine[:, k : k + 1] == columns).astype(jnp.int32)
        adj[at, :] = total.astype(f32).astype(bf16)
        return carry

    lax.fori_loop(0, n // GROUP, fill, 0)
    for j in range(3):
        at = pl.ds(j * n, n)
        adj_t[at, :] = adj[:, at].T

    bsend[...] = jnp.zeros_like(bsend)
    for c in range(chunks):
        fwd(0, c).wait_recv()
        fwd(1, c).wait_recv()
        root = inverse_root[...]
        summed = matmul(adj[...], window[c]) + window[c, pl.ds(n, n), :].astype(f32)
        pre = root * summed + bias[:, cols(c)]
        gate = jax.nn.sigmoid(pre)
        grad_pre = out_grad[:, cols(c)].astype(f32) * gate * (1.0 + pre * (1.0 - gate))
        grad_scaled = (grad_pre * root).astype(bf16)
        part_out[0, c] = matmul(adj_t[pl.ds(0, n), :], grad_scaled).astype(bf16)
        bwd(0, c).start()
        part_out[1, c] = matmul(adj_t[pl.ds(2 * n, n), :], grad_scaled).astype(bf16)
        bwd(1, c).start()
        own[c] = matmul(adj_t[pl.ds(n, n), :], grad_scaled) + grad_scaled.astype(f32)
        hidden[:, cols(c)] = (pre * gate).astype(bf16)
        bsend[pl.ds(c, 1), :] = jnp.sum(grad_pre, axis=0, keepdims=True)
    each(rows_n, lambda d: bcopy(d).start())

    def share_rows(c):
        each(rows_n, lambda d: wcopy(c, d).wait_recv())
        total = wsend[c, pl.ds(pl.multiple_of(r * share, share), share), :].astype(f32)
        for d in range(1, rows_n):
            total = total + wrecv[c, d].astype(f32)
        zbuf[c, z] = total.astype(bf16)
        each(feat_n, lambda d: zcopy(c, d).start())

    for c in range(chunks):
        bwd(0, c).wait_recv()
        bwd(1, c).wait_recv()
        total = own[c] + part_in[0, c].astype(f32) + part_in[1, c].astype(f32)
        piece = (inverse_root[...] * total).astype(bf16)
        wsend[c] = matmul(features_t[...], piece).astype(bf16)
        each(rows_n, lambda d: wcopy(c, d).start())
        grad_proj[:, cols(c)] = piece
        if c == 0:
            each(rows_n, lambda d: bcopy(d).wait_recv())
            total_bias = bsend[...]
            for d in range(1, rows_n):
                total_bias = total_bias + brecv[d]
            bz[z] = total_bias
            each(feat_n, lambda d: bzcopy(d).start())
        else:
            share_rows(c - 1)

    input_grad[...] = lax.dot_general(
        grad_proj[...], weight[...], (((1,), (1,)), ((), ())), preferred_element_type=f32
    ).astype(bf16)
    share_rows(chunks - 1)
    each(feat_n, lambda d: bzcopy(d).wait_recv())
    total_bias = bz[0]
    for p in range(1, feat_n):
        total_bias = total_bias + bz[p]
    bias_grad[...] = total_bias * scale
    for c in range(chunks):
        each(feat_n, lambda d: zcopy(c, d).wait_recv())
        total = zbuf[c, 0].astype(f32)
        for p in range(1, feat_n):
            total = total + zbuf[c, p].astype(f32)
        weight_grad[:, cols(c)] = total * scale

    for c in range(chunks):
        for side in range(2):
            fwd(side, c).wait_send()
            bwd(side, c).wait_send()
        each(rows_n, lambda d: wcopy(c, d).wait_send())
        each(feat_n, lambda d: zcopy(c, d).wait_send())
    each(rows_n, lambda d: bcopy(d).wait_send())
    each(feat_n, lambda d: bzcopy(d).wait_send())


def local(features, weight, layer_bias, block_cols, neighbours, row_counts, out_grad):
    n, width = features.shape
    tile_count, slot_count = block_cols.shape
    tile_rows = n // tile_count
    slots = neighbours.shape[1]
    rows_n, feat_n = lax.axis_size("rows"), lax.axis_size("feat")
    devices = rows_n * feat_n
    scale = 1.0 / math.sqrt(n * devices)
    chunks = width // LANES
    share = width // rows_n

    window_start = (lax.axis_index(("rows", "feat")) - 1) * tile_count
    local_slot = jnp.mod(block_cols - window_start, tile_count * devices)
    used = jnp.arange(slots, dtype=jnp.int32)[None, :] < row_counts[:, None]
    named = neighbours // tile_rows
    base = jnp.zeros_like(neighbours)
    for s in range(slot_count):
        base = jnp.where(named == s, jnp.repeat(local_slot[:, s], tile_rows)[:, None], base)
    keys = jnp.where(used, base * tile_rows + neighbours % tile_rows, -1)
    inverse_root = lax.rsqrt(1.0 + row_counts.astype(f32))[:, None]

    vmem = pl.BlockSpec(memory_space=pltpu.VMEM)
    bias_rows = max(8, chunks)
    dma = pltpu.SemaphoreType.DMA
    hidden, input_grad, weight_grad, bias_grad = pl.pallas_call(
        functools.partial(kernel, rows_n, feat_n, scale),
        out_shape=(
            jax.ShapeDtypeStruct((n, width), bf16),
            jax.ShapeDtypeStruct((n, width), bf16),
            jax.ShapeDtypeStruct((share, width), f32),
            jax.ShapeDtypeStruct((bias_rows, LANES), f32),
        ),
        in_specs=[vmem] * 6,
        out_specs=(vmem,) * 4,
        scratch_shapes=[
            pltpu.VMEM((chunks, 3 * n, LANES), bf16),
            pltpu.VMEM((n, 3 * n), bf16),
            pltpu.VMEM((3 * n, n), bf16),
            pltpu.VMEM((width, n), bf16),
            pltpu.VMEM((2, chunks, n, LANES), bf16),
            pltpu.VMEM((2, chunks, n, LANES), bf16),
            pltpu.VMEM((chunks, n, LANES), f32),
            pltpu.VMEM((n, width), bf16),
            pltpu.VMEM((chunks, width, LANES), bf16),
            pltpu.VMEM((chunks, rows_n, share, LANES), bf16),
            pltpu.VMEM((chunks, feat_n, share, LANES), bf16),
            pltpu.VMEM((bias_rows, LANES), f32),
            pltpu.VMEM((rows_n, bias_rows, LANES), f32),
            pltpu.VMEM((feat_n, bias_rows, LANES), f32),
            dma((2, chunks)), dma((2, chunks)), dma((2, chunks)), dma((2, chunks)),
            dma((chunks, rows_n)), dma((chunks, rows_n)),
            dma((chunks, feat_n)), dma((chunks, feat_n)),
            dma((rows_n,)), dma((rows_n,)), dma((feat_n,)), dma((feat_n,)),
        ],
        compiler_params=pltpu.CompilerParams(
            collective_id=0, has_side_effects=True, vmem_limit_bytes=48 * 2**20
        ),
        cost_estimate=pl.CostEstimate(
            flops=18 * n * width * width, bytes_accessed=12 * n * width, transcendentals=n * width
        ),
    )(features, weight, layer_bias[None, :], out_grad, keys, inverse_root)
    part_bias = lax.dynamic_slice_in_dim(
        bias_grad.reshape(-1), lax.axis_index("rows") * share, share, 0
    )
    return hidden, input_grad, weight_grad, part_bias


def solution(mesh):
    in_specs = (
        P(("rows", "feat"), None),
        P(),
        P(),
        P(("rows", "feat"), None),
        P(("rows", "feat"), None),
        P(("rows", "feat")),
        P(("rows", "feat"), None),
    )
    out_specs = (P(("rows", "feat"), None), P(("rows", "feat"), None), P("rows", None), P("rows"))
    return jax.shard_map(local, mesh=mesh, in_specs=in_specs, out_specs=out_specs, check_vma=False)
```

```python
import functools
import math

import jax
import jax.numpy as jnp
from jax import lax
from jax.experimental import pallas as pl
from jax.experimental.pallas import tpu as pltpu
from jax.sharding import PartitionSpec as P

LANES = 128
f32 = jnp.float32
bf16 = jnp.bfloat16


def matmul(a, b):
    return jnp.dot(a, b, preferred_element_type=f32)


def kernel(
    rows_n, feat_n, scale,
    features_hbm, weight_hbm, out_grad_hbm, neighbours_hbm, bias, counts, block_cols,
    hidden, input_grad, weight_grad, bias_grad,
    window, adj, adj_t, features_t, part_out, part_in, own, grad_proj,
    wsend, wrecv, zbuf, bsend, brecv, bz,
    features, weight, out_grad, neighbours, keys, inverse_root, load_sem,
    fwd_send, fwd_recv, bwd_send, bwd_recv, ws_sem, wr_sem, zs_sem, zr_sem,
    bs_sem, br_sem, bzs_sem, bzr_sem,
):
    n = features.shape[0]
    chunks = window.shape[0]
    share = weight_grad.shape[0]
    r = lax.axis_index("rows")
    z = lax.axis_index("feat")
    count = rows_n * feat_n
    me = r * feat_n + z
    prev = lax.rem(me + count - 1, count)
    succ = lax.rem(me + 1, count)
    sides = (
        {"rows": lax.div(prev, feat_n), "feat": lax.rem(prev, feat_n)},
        {"rows": lax.div(succ, feat_n), "feat": lax.rem(succ, feat_n)},
    )

    def row_peer(d):
        return {"rows": lax.rem(r + d, rows_n), "feat": z}

    def feat_peer(d):
        return {"rows": r, "feat": lax.rem(z + d, feat_n)}

    def remote(src, dst, send, recv, device):
        return pltpu.make_async_remote_copy(
            src_ref=src, dst_ref=dst, send_sem=send, recv_sem=recv,
            device_id=device, device_id_type=pl.DeviceIdType.MESH,
        )

    def each(size, act):
        def body(d, carry):
            act(d)
            return carry
        lax.fori_loop(1, size, body, 0)

    def cols(c):
        return pl.ds(c * LANES, LANES)

    def fwd(side, c):
        place = pl.ds(2 * n if side == 0 else 0, n)
        return remote(
            window.at[c, pl.ds(n, n)], window.at[c, place],
            fwd_send.at[side, c], fwd_recv.at[side, c], sides[side],
        )

    def bwd(side, c):
        return remote(
            part_out.at[side, c], part_in.at[side, c],
            bwd_send.at[side, c], bwd_recv.at[side, c], sides[side],
        )

    def wcopy(c, d):
        peer = row_peer(d)
        start = pl.multiple_of(peer["rows"] * share, share)
        return remote(
            wsend.at[c, pl.ds(start, share)], wrecv.at[c, d], ws_sem.at[c, d], wr_sem.at[c, d], peer
        )

    def zcopy(c, d):
        return remote(zbuf.at[c, z], zbuf.at[c, z], zs_sem.at[c, d], zr_sem.at[c, d], feat_peer(d))

    def bcopy(d):
        return remote(bsend, brecv.at[d], bs_sem.at[d], br_sem.at[d], row_peer(d))

    def bzcopy(d):
        return remote(bz.at[z], bz.at[z], bzs_sem.at[d], bzr_sem.at[d], feat_peer(d))

    barrier = pltpu.get_barrier_semaphore()

    def greet(device):
        pl.semaphore_signal(
            barrier, inc=1, device_id=device, device_id_type=pl.DeviceIdType.MESH
        )

    greet(sides[0])
    greet(sides[1])
    each(rows_n, lambda d: greet(row_peer(d)))
    each(feat_n, lambda d: greet(feat_peer(d)))

    loads = [
        pltpu.make_async_copy(src, dst, load_sem.at[i])
        for i, (src, dst) in enumerate(
            (
                (features_hbm, features),
                (weight_hbm, weight),
                (neighbours_hbm, neighbours),
                (out_grad_hbm, out_grad),
            )
        )
    ]
    for load in loads:
        load.start()
    root_row = lax.rsqrt(1.0 + counts[...].astype(f32))
    inverse_root[...] = jnp.broadcast_to(root_row, (LANES, n)).T
    loads[0].wait()
    loads[1].wait()

    for c in range(chunks):
        product = matmul(features[...], weight[:, cols(c)])
        window[c, pl.ds(n, n), :] = (product * inverse_root[...]).astype(bf16)
        if c == 0:
            pl.semaphore_wait(barrier, rows_n + feat_n)
        fwd(0, c).start()
        fwd(1, c).start()

    features_t[...] = features[...].T
    loads[2].wait()
    tile_count, slot_count = block_cols.shape
    all_tiles = tile_count * count
    slots = neighbours.shape[0]
    slot_ids = lax.broadcasted_iota(jnp.int32, (slots, LANES), 0)
    row_ids = lax.broadcasted_iota(jnp.int32, (LANES, LANES), 0)
    for t in range(tile_count):
        named = neighbours[:, cols(t)] // LANES
        place = neighbours[:, cols(t)] - named * LANES
        base = jnp.zeros_like(named)
        for s in range(slot_count):
            tile = lax.rem(block_cols[t, s] - (me - 1) * tile_count + all_tiles, all_tiles)
            base = jnp.where(named == s, tile, base)
        used = slot_ids < counts[:, cols(t)]
        keys[:, cols(t)] = jnp.where(used, base * LANES + place, -1)

        def fill(j, carry):
            start = pl.multiple_of(j * LANES, LANES)
            mine = keys[:, cols(t)] - start
            total = jnp.zeros((LANES, LANES), jnp.int32)
            for k in range(slots):
                total = total + (mine[k : k + 1, :] == row_ids).astype(jnp.int32)
            adj_t[pl.ds(start, LANES), cols(t)] = total.astype(f32).astype(bf16)
            return carry

        lax.fori_loop(0, 3 * n // LANES, fill, 0)
    for j in range(3):
        at = pl.ds(j * n, n)
        adj[:, at] = adj_t[at, :].T
    loads[3].wait()

    bsend[...] = jnp.zeros_like(bsend)
    for c in range(chunks):
        fwd(0, c).wait_recv()
        fwd(1, c).wait_recv()
        root = inverse_root[...]
        summed = matmul(adj[...], window[c]) + window[c, pl.ds(n, n), :].astype(f32)
        pre = root * summed + bias[:, cols(c)]
        gate = jax.nn.sigmoid(pre)
        grad_pre = out_grad[:, cols(c)].astype(f32) * gate * (1.0 + pre * (1.0 - gate))
        grad_scaled = (grad_pre * root).astype(bf16)
        part_out[0, c] = matmul(adj_t[pl.ds(0, n), :], grad_scaled).astype(bf16)
        bwd(0, c).start()
        part_out[1, c] = matmul(adj_t[pl.ds(2 * n, n), :], grad_scaled).astype(bf16)
        bwd(1, c).start()
        own[c] = matmul(adj_t[pl.ds(n, n), :], grad_scaled) + grad_scaled.astype(f32)
        hidden[:, cols(c)] = (pre * gate).astype(bf16)
        bsend[pl.ds(c, 1), :] = jnp.sum(grad_pre, axis=0, keepdims=True)
    each(rows_n, lambda d: bcopy(d).start())

    def share_rows(c):
        each(rows_n, lambda d: wcopy(c, d).wait_recv())
        total = wsend[c, pl.ds(pl.multiple_of(r * share, share), share), :].astype(f32)
        for d in range(1, rows_n):
            total = total + wrecv[c, d].astype(f32)
        zbuf[c, z] = total.astype(bf16)
        each(feat_n, lambda d: zcopy(c, d).start())

    for c in range(chunks):
        bwd(0, c).wait_recv()
        bwd(1, c).wait_recv()
        total = own[c] + part_in[0, c].astype(f32) + part_in[1, c].astype(f32)
        piece = (inverse_root[...] * total).astype(bf16)
        wsend[c] = matmul(features_t[...], piece).astype(bf16)
        each(rows_n, lambda d: wcopy(c, d).start())
        grad_proj[:, cols(c)] = piece
        if c == 0:
            each(rows_n, lambda d: bcopy(d).wait_recv())
            total_bias = bsend[...]
            for d in range(1, rows_n):
                total_bias = total_bias + brecv[d]
            bz[z] = total_bias
            each(feat_n, lambda d: bzcopy(d).start())
        else:
            share_rows(c - 1)

    input_grad[...] = lax.dot_general(
        grad_proj[...], weight[...], (((1,), (1,)), ((), ())), preferred_element_type=f32
    ).astype(bf16)
    share_rows(chunks - 1)
    each(feat_n, lambda d: bzcopy(d).wait_recv())
    total_bias = bz[0]
    for p in range(1, feat_n):
        total_bias = total_bias + bz[p]
    bias_grad[...] = total_bias * scale
    for c in range(chunks):
        each(feat_n, lambda d: zcopy(c, d).wait_recv())
        total = zbuf[c, 0].astype(f32)
        for p in range(1, feat_n):
            total = total + zbuf[c, p].astype(f32)
        weight_grad[:, cols(c)] = total * scale

    for c in range(chunks):
        for side in range(2):
            fwd(side, c).wait_send()
            bwd(side, c).wait_send()
        each(rows_n, lambda d: wcopy(c, d).wait_send())
        each(feat_n, lambda d: zcopy(c, d).wait_send())
    each(rows_n, lambda d: bcopy(d).wait_send())
    each(feat_n, lambda d: bzcopy(d).wait_send())


def local(features, weight, layer_bias, block_cols, neighbours, row_counts, out_grad):
    n, width = features.shape
    slots = neighbours.shape[1]
    rows_n, feat_n = lax.axis_size("rows"), lax.axis_size("feat")
    devices = rows_n * feat_n
    scale = 1.0 / math.sqrt(n * devices)
    chunks = width // LANES
    share = width // rows_n

    vmem = pl.BlockSpec(memory_space=pltpu.VMEM)
    anywhere = pl.BlockSpec(memory_space=pltpu.HBM)
    bias_rows = max(8, chunks)
    dma = pltpu.SemaphoreType.DMA
    hidden, input_grad, weight_grad, bias_grad = pl.pallas_call(
        functools.partial(kernel, rows_n, feat_n, scale),
        out_shape=(
            jax.ShapeDtypeStruct((n, width), bf16),
            jax.ShapeDtypeStruct((n, width), bf16),
            jax.ShapeDtypeStruct((share, width), f32),
            jax.ShapeDtypeStruct((bias_rows, LANES), f32),
        ),
        in_specs=[anywhere] * 4 + [vmem] * 2 + [pl.BlockSpec(memory_space=pltpu.SMEM)],
        out_specs=(vmem,) * 4,
        scratch_shapes=[
            pltpu.VMEM((chunks, 3 * n, LANES), bf16),
            pltpu.VMEM((n, 3 * n), bf16),
            pltpu.VMEM((3 * n, n), bf16),
            pltpu.VMEM((width, n), bf16),
            pltpu.VMEM((2, chunks, n, LANES), bf16),
            pltpu.VMEM((2, chunks, n, LANES), bf16),
            pltpu.VMEM((chunks, n, LANES), f32),
            pltpu.VMEM((n, width), bf16),
            pltpu.VMEM((chunks, width, LANES), bf16),
            pltpu.VMEM((chunks, rows_n, share, LANES), bf16),
            pltpu.VMEM((chunks, feat_n, share, LANES), bf16),
            pltpu.VMEM((bias_rows, LANES), f32),
            pltpu.VMEM((rows_n, bias_rows, LANES), f32),
            pltpu.VMEM((feat_n, bias_rows, LANES), f32),
            pltpu.VMEM((n, width), bf16),
            pltpu.VMEM((width, width), bf16),
            pltpu.VMEM((n, width), bf16),
            pltpu.VMEM((slots, n), jnp.int32),
            pltpu.VMEM((slots, n), jnp.int32),
            pltpu.VMEM((n, LANES), f32),
            dma((4,)),
            dma((2, chunks)), dma((2, chunks)), dma((2, chunks)), dma((2, chunks)),
            dma((chunks, rows_n)), dma((chunks, rows_n)),
            dma((chunks, feat_n)), dma((chunks, feat_n)),
            dma((rows_n,)), dma((rows_n,)), dma((feat_n,)), dma((feat_n,)),
        ],
        compiler_params=pltpu.CompilerParams(
            collective_id=0, has_side_effects=True, vmem_limit_bytes=63 * 2**20
        ),
        cost_estimate=pl.CostEstimate(
            flops=18 * n * width * width, bytes_accessed=12 * n * width, transcendentals=n * width
        ),
    )(features, weight, out_grad, neighbours.T, layer_bias[None, :], row_counts[None, :], block_cols)
    part_bias = lax.dynamic_slice_in_dim(
        bias_grad.reshape(-1), lax.axis_index("rows") * share, share, 0
    )
    return hidden, input_grad, weight_grad, part_bias


def solution(mesh):
    in_specs = (
        P(("rows", "feat"), None),
        P(),
        P(),
        P(("rows", "feat"), None),
        P(("rows", "feat"), None),
        P(("rows", "feat")),
        P(("rows", "feat"), None),
    )
    out_specs = (P(("rows", "feat"), None), P(("rows", "feat"), None), P("rows", None), P("rows"))
    return jax.shard_map(local, mesh=mesh, in_specs=in_specs, out_specs=out_specs, check_vma=False)
```

```python
import functools
import math

import jax
import jax.numpy as jnp
from jax import lax
from jax.experimental import pallas as pl
from jax.experimental.pallas import tpu as pltpu
from jax.sharding import PartitionSpec as P

LANES = 128
f32 = jnp.float32
bf16 = jnp.bfloat16


def matmul(a, b):
    return jnp.dot(a, b, preferred_element_type=f32)


def kernel(
    rows_n, feat_n, scale,
    features_hbm, weight_hbm, out_grad_hbm, neighbours_hbm, bias, counts, block_cols,
    hidden, input_grad, weight_grad, bias_grad,
    window, adj, adj_t, features_t, part_out, part_in, own, grad_proj,
    wsend, wrecv, zbuf, bsend, brecv, bz,
    features, weight, out_grad, neighbours, keys, inverse_root, load_sem,
    fwd_send, fwd_recv, bwd_send, bwd_recv, ws_sem, wr_sem, zs_sem, zr_sem,
    bs_sem, br_sem, bzs_sem, bzr_sem,
):
    n = features.shape[0]
    chunks = window.shape[0]
    share = weight_grad.shape[0]
    r = lax.axis_index("rows")
    z = lax.axis_index("feat")
    count = rows_n * feat_n
    me = r * feat_n + z
    prev = lax.rem(me + count - 1, count)
    succ = lax.rem(me + 1, count)
    sides = (
        {"rows": lax.div(prev, feat_n), "feat": lax.rem(prev, feat_n)},
        {"rows": lax.div(succ, feat_n), "feat": lax.rem(succ, feat_n)},
    )

    def row_peer(d):
        return {"rows": lax.rem(r + d, rows_n), "feat": z}

    def feat_peer(d):
        return {"rows": r, "feat": lax.rem(z + d, feat_n)}

    def remote(src, dst, send, recv, device):
        return pltpu.make_async_remote_copy(
            src_ref=src, dst_ref=dst, send_sem=send, recv_sem=recv,
            device_id=device, device_id_type=pl.DeviceIdType.MESH,
        )

    def each(size, act):
        def body(d, carry):
            act(d)
            return carry
        lax.fori_loop(1, size, body, 0)

    def cols(c):
        return pl.ds(c * LANES, LANES)

    def fwd(side, c):
        place = pl.ds(2 * n if side == 0 else 0, n)
        return remote(
            window.at[c, pl.ds(n, n)], window.at[c, place],
            fwd_send.at[side, c], fwd_recv.at[side, c], sides[side],
        )

    def bwd(side, c):
        return remote(
            part_out.at[side, c], part_in.at[side, c],
            bwd_send.at[side, c], bwd_recv.at[side, c], sides[side],
        )

    def wcopy(c, d):
        peer = row_peer(d)
        start = pl.multiple_of(peer["rows"] * share, share)
        return remote(
            wsend.at[c, pl.ds(start, share)], wrecv.at[c, d], ws_sem.at[c, d], wr_sem.at[c, d], peer
        )

    def zcopy(c, d):
        return remote(zbuf.at[c, z], zbuf.at[c, z], zs_sem.at[c, d], zr_sem.at[c, d], feat_peer(d))

    def bcopy(d):
        return remote(bsend, brecv.at[d], bs_sem.at[d], br_sem.at[d], row_peer(d))

    def bzcopy(d):
        return remote(bz.at[z], bz.at[z], bzs_sem.at[d], bzr_sem.at[d], feat_peer(d))

    barrier = pltpu.get_barrier_semaphore()

    def greet(device):
        pl.semaphore_signal(
            barrier, inc=1, device_id=device, device_id_type=pl.DeviceIdType.MESH
        )

    greet(sides[0])
    greet(sides[1])
    each(rows_n, lambda d: greet(row_peer(d)))
    each(feat_n, lambda d: greet(feat_peer(d)))

    loads = [
        pltpu.make_async_copy(src, dst, load_sem.at[i])
        for i, (src, dst) in enumerate(
            (
                (features_hbm, features),
                (weight_hbm, weight),
                (neighbours_hbm, neighbours),
                (out_grad_hbm, out_grad),
            )
        )
    ]
    for load in loads:
        load.start()
    root_row = lax.rsqrt(1.0 + counts[...].astype(f32))
    inverse_root[...] = jnp.broadcast_to(root_row, (LANES, n)).T
    loads[0].wait()
    loads[1].wait()

    for c in range(chunks):
        product = matmul(features[...], weight[:, cols(c)])
        window[c, pl.ds(n, n), :] = (product * inverse_root[...]).astype(bf16)
        if c == 0:
            pl.semaphore_wait(barrier, rows_n + feat_n)
        fwd(0, c).start()
        fwd(1, c).start()

    features_t[...] = features[...].T
    loads[2].wait()
    tile_count, slot_count = block_cols.shape
    all_tiles = tile_count * count
    slots = neighbours.shape[0]
    slot_ids = lax.broadcasted_iota(jnp.int32, (slots, LANES), 0)
    row_ids = lax.broadcasted_iota(jnp.int32, (LANES, LANES), 0)
    for t in range(tile_count):
        named = neighbours[:, cols(t)] // LANES
        place = neighbours[:, cols(t)] - named * LANES
        base = jnp.zeros_like(named)
        for s in range(slot_count):
            tile = lax.rem(block_cols[t, s] - (me - 1) * tile_count + all_tiles, all_tiles)
            base = jnp.where(named == s, tile, base)
        used = slot_ids < counts[:, cols(t)]
        keys[:, cols(t)] = jnp.where(used, base * LANES + place, -1)

        def fill(j, carry):
            start = pl.multiple_of(j * LANES, LANES)
            mine = keys[:, cols(t)] - start
            total = jnp.zeros((LANES, LANES), jnp.int32)
            for k in range(slots):
                total = total + (mine[k : k + 1, :] == row_ids).astype(jnp.int32)
            adj_t[pl.ds(start, LANES), cols(t)] = total.astype(f32).astype(bf16)
            return carry

        lax.fori_loop(0, 3 * n // LANES, fill, 0)
    for j in range(3):
        at = pl.ds(j * n, n)
        adj[:, at] = adj_t[at, :].T
    loads[3].wait()

    bsend[...] = jnp.zeros_like(bsend)
    for c in range(chunks):
        fwd(0, c).wait_recv()
        fwd(1, c).wait_recv()
        root = inverse_root[...]
        summed = matmul(adj[...], window[c]) + window[c, pl.ds(n, n), :].astype(f32)
        pre = root * summed + bias[:, cols(c)]
        gate = jax.nn.sigmoid(pre)
        grad_pre = out_grad[:, cols(c)].astype(f32) * gate * (1.0 + pre * (1.0 - gate))
        grad_scaled = (grad_pre * root).astype(bf16)
        part_out[0, c] = matmul(adj_t[pl.ds(0, n), :], grad_scaled).astype(bf16)
        bwd(0, c).start()
        part_out[1, c] = matmul(adj_t[pl.ds(2 * n, n), :], grad_scaled).astype(bf16)
        bwd(1, c).start()
        own[c] = matmul(adj_t[pl.ds(n, n), :], grad_scaled) + grad_scaled.astype(f32)
        hidden[:, cols(c)] = (pre * gate).astype(bf16)
        bsend[pl.ds(c, 1), :] = jnp.sum(grad_pre, axis=0, keepdims=True)
    each(rows_n, lambda d: bcopy(d).start())

    def share_rows(c):
        each(rows_n, lambda d: wcopy(c, d).wait_recv())
        total = wsend[c, pl.ds(pl.multiple_of(r * share, share), share), :].astype(f32)
        for d in range(1, rows_n):
            total = total + wrecv[c, d].astype(f32)
        zbuf[c, z] = total.astype(bf16)
        each(feat_n, lambda d: zcopy(c, d).start())

    for c in range(chunks):
        bwd(0, c).wait_recv()
        bwd(1, c).wait_recv()
        total = own[c] + part_in[0, c].astype(f32) + part_in[1, c].astype(f32)
        piece = (inverse_root[...] * total).astype(bf16)
        wsend[c] = matmul(features_t[...], piece).astype(bf16)
        each(rows_n, lambda d: wcopy(c, d).start())
        grad_proj[:, cols(c)] = piece
        if c == 0:
            each(rows_n, lambda d: bcopy(d).wait_recv())
            total_bias = bsend[...]
            for d in range(1, rows_n):
                total_bias = total_bias + brecv[d]
            bz[z] = total_bias
            each(feat_n, lambda d: bzcopy(d).start())
        else:
            share_rows(c - 1)

    input_grad[...] = lax.dot_general(
        grad_proj[...], weight[...], (((1,), (1,)), ((), ())), preferred_element_type=f32
    ).astype(bf16)
    share_rows(chunks - 1)
    each(feat_n, lambda d: bzcopy(d).wait_recv())
    total_bias = bz[0]
    for p in range(1, feat_n):
        total_bias = total_bias + bz[p]
    bias_grad[...] = total_bias * scale
    for c in range(chunks):
        each(feat_n, lambda d: zcopy(c, d).wait_recv())
        total = zbuf[c, 0].astype(f32)
        for p in range(1, feat_n):
            total = total + zbuf[c, p].astype(f32)
        weight_grad[:, cols(c)] = total * scale

    for c in range(chunks):
        for side in range(2):
            fwd(side, c).wait_send()
            bwd(side, c).wait_send()
        each(rows_n, lambda d: wcopy(c, d).wait_send())
        each(feat_n, lambda d: zcopy(c, d).wait_send())
    each(rows_n, lambda d: bcopy(d).wait_send())
    each(feat_n, lambda d: bzcopy(d).wait_send())


def local(features, weight, layer_bias, block_cols, neighbours, row_counts, out_grad):
    n, width = features.shape
    slots = neighbours.shape[1]
    rows_n, feat_n = lax.axis_size("rows"), lax.axis_size("feat")
    devices = rows_n * feat_n
    scale = 1.0 / math.sqrt(n * devices)
    chunks = width // LANES
    share = width // rows_n

    vmem = pl.BlockSpec(memory_space=pltpu.VMEM)
    anywhere = pl.BlockSpec(memory_space=pltpu.HBM)
    bias_rows = max(8, chunks)
    dma = pltpu.SemaphoreType.DMA
    hidden, input_grad, weight_grad, bias_grad = pl.pallas_call(
        functools.partial(kernel, rows_n, feat_n, scale),
        out_shape=(
            jax.ShapeDtypeStruct((n, width), bf16),
            jax.ShapeDtypeStruct((n, width), bf16),
            jax.ShapeDtypeStruct((share, width), f32),
            jax.ShapeDtypeStruct((bias_rows, LANES), f32),
        ),
        in_specs=[anywhere] * 4 + [vmem] * 2 + [pl.BlockSpec(memory_space=pltpu.SMEM)],
        out_specs=(vmem,) * 4,
        scratch_shapes=[
            pltpu.VMEM((chunks, 3 * n, LANES), bf16),
            pltpu.VMEM((n, 3 * n), bf16),
            pltpu.VMEM((3 * n, n), bf16),
            pltpu.VMEM((width, n), bf16),
            pltpu.VMEM((2, chunks, n, LANES), bf16),
            pltpu.VMEM((2, chunks, n, LANES), bf16),
            pltpu.VMEM((chunks, n, LANES), f32),
            pltpu.VMEM((n, width), bf16),
            pltpu.VMEM((chunks, width, LANES), bf16),
            pltpu.VMEM((chunks, rows_n, share, LANES), bf16),
            pltpu.VMEM((chunks, feat_n, share, LANES), bf16),
            pltpu.VMEM((bias_rows, LANES), f32),
            pltpu.VMEM((rows_n, bias_rows, LANES), f32),
            pltpu.VMEM((feat_n, bias_rows, LANES), f32),
            pltpu.VMEM((n, width), bf16),
            pltpu.VMEM((width, width), bf16),
            pltpu.VMEM((n, width), bf16),
            pltpu.VMEM((slots, n), jnp.int32),
            pltpu.VMEM((slots, n), jnp.int32),
            pltpu.VMEM((n, LANES), f32),
            dma((4,)),
            dma((2, chunks)), dma((2, chunks)), dma((2, chunks)), dma((2, chunks)),
            dma((chunks, rows_n)), dma((chunks, rows_n)),
            dma((chunks, feat_n)), dma((chunks, feat_n)),
            dma((rows_n,)), dma((rows_n,)), dma((feat_n,)), dma((feat_n,)),
        ],
        compiler_params=pltpu.CompilerParams(
            collective_id=0, has_side_effects=True, vmem_limit_bytes=48 * 2**20
        ),
        cost_estimate=pl.CostEstimate(
            flops=18 * n * width * width, bytes_accessed=12 * n * width, transcendentals=n * width
        ),
    )(features, weight, out_grad, neighbours.T, layer_bias[None, :], row_counts[None, :], block_cols)
    part_bias = lax.dynamic_slice_in_dim(
        bias_grad.reshape(-1), lax.axis_index("rows") * share, share, 0
    )
    return hidden, input_grad, weight_grad, part_bias


def solution(mesh):
    in_specs = (
        P(("rows", "feat"), None),
        P(),
        P(),
        P(("rows", "feat"), None),
        P(("rows", "feat"), None),
        P(("rows", "feat")),
        P(("rows", "feat"), None),
    )
    out_specs = (P(("rows", "feat"), None), P(("rows", "feat"), None), P("rows", None), P("rows"))
    return jax.shard_map(local, mesh=mesh, in_specs=in_specs, out_specs=out_specs, check_vma=False)
```
